32 devices in a mesh: replica: 2 (over x), expert: 16 (over z, y, core).
Axes of the slice: x: 2, y: 2, z: 4, core: 2. Of those that a mesh axis runs over, the one named last changes fastest.
Arguments:
- tokens: bfloat16 [4096, 2048], P(('replica', 'expert')), parts along dimension 0, may hold values from -6 to 6
- expert_ids: int32 [4096, 8], P(('replica', 'expert')), parts along dimension 0, may hold values from 0 to 31, all different within a row; in each aligned block of 128 rows (0 to 127, 128 to 255, ...) at most 64 rows name the same one
- gate_levels: int32 [4096, 8], P(('replica', 'expert')), parts along dimension 0, may hold values from 1 to 255
- gate_up: bfloat16 [32, 2048, 1536], P('expert'), may hold values from -0.125 to 0.125
- down_proj: bfloat16 [32, 768, 2048], P('expert'), may hold values from -0.21875 to 0.21875
Outputs:
- mixed: bfloat16 [4096, 2048], P(('replica', 'expert')), parts along dimension 0
The draws below stay inside these ranges and needn't reach their ends.
There are 2 independent parts, one for each index of `replica`. The reference program is written for one: setup_inputs(seed, part) draws one part's arguments, and reference() takes and returns one part's arrays. A program takes and returns all parts, laid end to end along the dimension named above; an argument that names none is the same for every part. Nothing has to cross between parts.
Inputs may be any that keep to these rules, and one draw needn't show every extreme that they name: `expert_ids`: each row names 8 different experts. Among the 128 rows of one device (aligned blocks), no expert is named by more than 64 rows, and in every draw some expert is named by exactly 64 rows of some device.
All inputs are finite; a program needn't handle non-finite values.
Results may differ from the reference program's by a relative error of at most 0.0057.
Values may be sent and summed in bfloat16 or wider, within the bound.
A program may use at most 128 MiB of HBM per device.

```python
import math
import jax
import jax.numpy as jnp
import numpy as np
from jax import lax

D = 2048
FF = 768
TOP = 8
TOK_DEV = 128
EXPERTS = 32
TOKENS = 2048
CAP = 64
N_EXPERT = 16


def touch_ends(result, own_key, least, high):
    spot = [jax.random.randint(jax.random.fold_in(own_key, axis), (), 0, length) for axis, length in enumerate(result.shape)]
    widest = result.shape.index(max(result.shape))
    neighbour = spot[:widest] + [(spot[widest] + 1) % result.shape[widest]] + spot[widest + 1:]
    return result.at[tuple(spot)].set(least).at[tuple(neighbour)].set(high)


def level_of(stream_key, shape, pieces, smallest, high):
    def one(dim, blocks):
        steps = jax.random.uniform(jax.random.fold_in(jax.random.fold_in(stream_key, 6), dim), (blocks,), jnp.float32, smallest / len(pieces), high / len(pieces))
        return jnp.repeat(jnp.exp(steps), shape[dim] // blocks).reshape((-1,) + (1,) * (len(shape) - dim - 1))

    level = one(*pieces[0])
    for cut in pieces[1:]:
        level = level * one(*cut)
    return level


def assign_block(key, own, number, rows, count, top, reach, lean):
    sequence = jax.random.permutation(key, count)
    crowded, common = portions_of(count, rows * top, reach, lean, True), portions_of(count, rows * top, reach, lean, False)
    places = jnp.arange(count)

    def named(lengths, offset_by):
        used = int((lengths > 0).sum())
        fixed = max(1, used // 4)
        shifted = fixed + (places - fixed + offset_by * (used - fixed)) % max(1, count - fixed)
        return jnp.zeros((count,), jnp.int32).at[sequence[jnp.where(places < fixed, places, shifted)]].set(jnp.asarray(lengths, jnp.int32))

    lengths = jnp.where(number % 4 == 0, named(crowded, number // 4), named(common, number - number // 4 - 1))
    mixed = jax.random.permutation(jax.random.fold_in(own, 3), count)
    donor, sink = mixed[0:count // 2 * 2:2], mixed[1:count // 2 * 2:2]
    slack = jnp.minimum(lengths[donor] - 1, reach - lengths[sink]) // 2
    slack = jnp.where((donor == sequence[0]) | (sink == sequence[0]) | (lengths[sink] == 0), 0, jnp.maximum(slack, 0))
    shifted = jax.random.randint(jax.random.fold_in(own, 4), (count // 2,), 0, 1 << 20) % (slack + 1)
    lengths = lengths.at[donor].add(-shifted).at[sink].add(shifted)
    members = jnp.searchsorted(jnp.cumsum(lengths), jnp.arange(rows * top), side="right").astype(jnp.int32)
    listing = members.reshape(top, rows).T
    listing = listing[jax.random.permutation(jax.random.fold_in(own, 1), rows)]
    offset_by = jax.random.randint(jax.random.fold_in(own, 2), (rows, 1), 0, top)
    return jnp.take_along_axis(listing, (jnp.arange(top)[None, :] + offset_by) % top, axis=1)


def portions_of(number_of, total, most, skew, full):
    portions = [(1 << 20) // math.isqrt(standing ** skew) + 1 for standing in range(1, number_of + 1)]
    largest = most if full else min(most, max(-(-total // number_of), total * portions[0] // sum(portions)))
    least = 1 if total - largest >= number_of - 1 else 0
    counts, spare = [largest] + [least] * (number_of - 1), total - largest - least * (number_of - 1)
    while spare > 0:
        candidates = [i for i in range(1, number_of) if counts[i] < largest] or [i for i in range(1, number_of) if counts[i] < most]
        mass, remaining = sum([portions[i] for i in candidates]), spare
        for i in candidates:
            addition = min(most - counts[i], max(1, remaining * portions[i] // mass), spare)
            counts[i] = counts[i] + addition
            spare = spare - addition
    return np.array(counts)


def scatter_about(key, extent, deviation, limit, shards=(), kind=jnp.bfloat16):
    values = jax.random.normal(key, extent, jnp.float32) * deviation
    if len(shards) > 0:
        values = level_of(key, extent, shards, -0.22, 0.18) * values
    return jnp.clip(values, min=-limit, max=limit).astype(kind)


def setup_inputs(seed: int = 0, part: int = 0) -> dict:
    key_list = jax.random.split(jax.random.key(seed), 6)
    part_splits = jax.random.split(jax.random.fold_in(key_list[5], part), 6)
    tokens = scatter_about(part_splits[0], (TOKENS, D), 1.0, 6.0, ((0, 16),))
    expert_ids_keys = jax.random.split(jax.random.fold_in(part_splits[1], 1), TOKENS // TOK_DEV)
    expert_ids_turns = jax.random.permutation(jax.random.fold_in(part_splits[1], 3), TOKENS // TOK_DEV)
    expert_ids = jax.vmap(lambda own, number: assign_block(jax.random.fold_in(part_splits[1], 2), own, number, TOK_DEV, EXPERTS, TOP, CAP, 2))(expert_ids_keys, expert_ids_turns).reshape((TOKENS, TOP))
    gate_levels = touch_ends(jax.random.randint(part_splits[2], (TOKENS, TOP), 1, 256), jax.random.fold_in(part_splits[2], 1), 1, 255).astype(jnp.int32)
    gate_up = scatter_about(key_list[3], (EXPERTS, D, 2 * FF), D ** -0.5, 0.125, ((0, 16),))
    down_proj = scatter_about(key_list[4], (EXPERTS, FF, D), FF ** -0.5, 0.21875, ((0, 16),))
    return dict(tokens=tokens, expert_ids=expert_ids, gate_levels=gate_levels, gate_up=gate_up, down_proj=down_proj)


def expert_output(rows, weight_in, weight_out):
    projected = jnp.dot(rows, weight_in, preferred_element_type=jnp.float32)
    half_width = weight_out.shape[0]
    hidden = (jax.nn.silu(projected[:, :half_width]) * projected[:, half_width:]).astype(jnp.bfloat16)
    return jnp.dot(hidden, weight_out, preferred_element_type=jnp.float32).astype(jnp.bfloat16)


def reference(tokens, expert_ids, gate_levels, gate_up, down_proj):
    flat_experts = expert_ids.reshape(-1).astype(jnp.int32)
    owner = (jnp.arange(TOKENS * TOP, dtype=jnp.int32) // TOP).astype(jnp.int32)
    weights = gate_levels.astype(jnp.float32)
    weights = weights / jnp.sum(weights, axis=1, keepdims=True)
    flat_weights = weights.reshape(-1)
    bound = N_EXPERT * CAP
    with_blank = jnp.concatenate([tokens, jnp.zeros((1, D), jnp.bfloat16)], axis=0)

    def per_expert(total, expert):
        chosen = flat_experts == expert
        order = (jnp.cumsum(chosen.astype(jnp.int32)) - 1).astype(jnp.int32)
        target = jnp.where(chosen, order, bound).astype(jnp.int32)
        rows = jnp.full((bound,), TOKENS, jnp.int32).at[target].set(owner, mode="drop")
        slot_weights = jnp.zeros((bound,), jnp.float32).at[target].set(flat_weights, mode="drop")
        output = expert_output(with_blank[rows], gate_up[expert], down_proj[expert])
        total = total.at[rows].add(slot_weights[:, None] * output.astype(jnp.float32))
        return total, None

    total, unused = lax.scan(per_expert, jnp.zeros((TOKENS + 1, D), jnp.float32), jnp.arange(EXPERTS, dtype=jnp.int32))
    return total[:TOKENS].astype(jnp.bfloat16)
```

```python
import jax
import jax.numpy as jnp
from jax import lax
from jax.sharding import PartitionSpec as P


def on_device(tokens, expert_ids, gate_levels, gate_up, down_proj):
    exp_dev = gate_up.shape[0]
    half = down_proj.shape[1]
    weights = gate_levels.astype(jnp.float32)
    weights = weights / jnp.sum(weights, axis=1, keepdims=True)
    all_tokens = lax.all_gather(tokens, "expert", axis=0, tiled=True)
    all_ids = lax.all_gather(expert_ids, "expert", axis=0, tiled=True)
    all_weights = lax.all_gather(weights, "expert", axis=0, tiled=True)
    first = lax.axis_index("expert") * exp_dev
    parts = []
    for expert in range(exp_dev):
        named = all_ids == first + expert
        share = jnp.sum(jnp.where(named, all_weights, 0.0), axis=1, keepdims=True)
        projected = jnp.dot(all_tokens, gate_up[expert], preferred_element_type=jnp.float32)
        hidden = jax.nn.silu(projected[:, :half]) * projected[:, half:]
        parts.append((hidden * share).astype(jnp.bfloat16))
    hidden = jnp.concatenate(parts, axis=1)
    down = down_proj.reshape(exp_dev * half, down_proj.shape[2])
    partial = jnp.dot(hidden, down, preferred_element_type=jnp.float32).astype(jnp.bfloat16)
    return lax.psum_scatter(partial, "expert", scatter_dimension=0, tiled=True)


def solution(mesh):
    rows = P(("replica", "expert"), None)
    return jax.shard_map(
        on_device,
        mesh=mesh,
        in_specs=(rows, rows, rows, P("expert", None, None), P("expert", None, None)),
        out_specs=rows,
        check_vma=False,
    )
```

```python
import functools
import jax
import jax.numpy as jnp
from jax import lax
from jax.sharding import PartitionSpec as P

PAD = 128
CUTS = 2


def apply_experts(packed, first, width, top, gate_up, down_proj):
    exp_dev, half = down_proj.shape[:2]
    rows = packed[:, :width]
    ids = packed[:, width : width + top].astype(jnp.int32)
    levels = packed[:, width + top : width + 2 * top].astype(jnp.float32)
    weights = levels / jnp.sum(levels, axis=1, keepdims=True)
    parts = []
    for expert in range(exp_dev):
        share = jnp.sum(jnp.where(ids == first + expert, weights, 0.0), axis=1, keepdims=True)
        projected = jnp.dot(rows, gate_up[expert], preferred_element_type=jnp.float32)
        hidden = jax.nn.silu(projected[:, :half]) * projected[:, half:]
        parts.append((hidden * share).astype(jnp.bfloat16))
    down = down_proj.reshape(exp_dev * half, width)
    return jnp.dot(
        jnp.concatenate(parts, axis=1), down, preferred_element_type=jnp.float32
    ).astype(jnp.bfloat16)


def add(*terms):
    total = terms[0].astype(jnp.float32)
    for term in terms[1:]:
        total = total + term.astype(jnp.float32)
    return total.astype(jnp.bfloat16)


def on_device(y_size, tokens, expert_ids, gate_levels, gate_up, down_proj):
    tok_dev, width = tokens.shape
    top = expert_ids.shape[1]
    n = lax.axis_size("expert")
    z_size = n // (2 * y_size)
    me = lax.axis_index("expert")
    core, y, z = me % 2, (me // 2) % y_size, me // (2 * y_size)
    first = me * gate_up.shape[0]

    packed = jnp.concatenate(
        [
            tokens,
            expert_ids.astype(jnp.bfloat16),
            gate_levels.astype(jnp.bfloat16),
            jnp.zeros((tok_dev, PAD - 2 * top), jnp.bfloat16),
        ],
        axis=1,
    )
    gathered = lax.all_gather(packed, "expert", axis=0, tiled=True)
    gathered = gathered.reshape(z_size, y_size, 2, tok_dev, width + PAD)

    def group(y_to, core_to, after):
        rows = lax.dynamic_slice(
            gathered, (0, y_to, core_to, 0, 0), (z_size, 1, 1, tok_dev, width + PAD)
        ).reshape(z_size * tok_dev, width + PAD)
        if after is not None:
            rows, after = lax.optimization_barrier((rows, after))
        part = apply_experts(rows, first, width, top, gate_up, down_proj)
        return part, after

    core_pairs = [(i, i ^ 1) for i in range(n)]
    y_pairs = [(i, i ^ 2) for i in range(n)]
    from_y = None
    last = None
    for y_to in [(y + step) % y_size for step in range(1, y_size)] + [y]:
        away, last = group(y_to, 1 - core, last)
        arrived = lax.ppermute(away, "expert", core_pairs)
        kept, _ = group(y_to, core, away)
        last = lax.optimization_barrier(kept)
        if y_to is y:
            terms = [last, arrived] + ([] if from_y is None else [from_y])
            total = add(*terms)
        else:
            from_y = lax.ppermute(add(last, arrived), "expert", y_pairs)

    total = total.reshape(z_size, tok_dev, width)
    step_z = 2 * y_size
    columns = width // CUTS
    outs = []
    for cut in range(CUTS):
        own = total[:, :, cut * columns : (cut + 1) * columns]

        def block(at):
            return lax.dynamic_index_in_dim(own, jnp.clip(at, 0, z_size - 1), 0, keepdims=False)

        up, down = None, None
        for step in range(z_size - 1):
            reach = z_size - 1 - step
            up_block, down_block = block(z + reach), block(z - reach)
            up = up_block if up is None else add(up, up_block)
            down = down_block if down is None else add(down, down_block)
            up_pairs = [(i, i + step_z) for i in range(n) if i // step_z + reach < z_size]
            down_pairs = [(i, i - step_z) for i in range(n) if i // step_z >= reach]
            up = lax.ppermute(up, "expert", up_pairs)
            down = lax.ppermute(down, "expert", down_pairs)
        outs.append(add(block(z), up, down) if z_size > 1 else own[0])
    return jnp.concatenate(outs, axis=1)


def solution(mesh):
    y_size = max(1, 4 // mesh.shape["replica"])
    rows = P(("replica", "expert"), None)
    return jax.shard_map(
        functools.partial(on_device, y_size),
        mesh=mesh,
        in_specs=(rows, rows, rows, P("expert", None, None), P("expert", None, None)),
        out_specs=rows,
        check_vma=False,
    )
```

```python
import functools
import jax
import jax.numpy as jnp
from jax import lax
from jax.sharding import PartitionSpec as P

LANES = 128
CUTS = 2


def apply_experts(rows, shares, gate_up, down_proj):
    exp_dev, half, width = down_proj.shape
    parts = []
    for expert in range(exp_dev):
        projected = jnp.dot(rows, gate_up[expert], preferred_element_type=jnp.float32)
        hidden = jax.nn.silu(projected[:, :half]) * projected[:, half:]
        parts.append((hidden * shares[:, expert : expert + 1]).astype(jnp.bfloat16))
    down = down_proj.reshape(exp_dev * half, width)
    return jnp.dot(
        jnp.concatenate(parts, axis=1), down, preferred_element_type=jnp.float32
    ).astype(jnp.bfloat16)


def gather_small(small, me, n):
    held = small[None]
    bit = 1
    while bit < n:
        other = lax.ppermute(held, "expert", [(i, i ^ bit) for i in range(n)])
        held = jnp.concatenate([held, other], axis=0)
        bit *= 2
    return jnp.take(held, me ^ jnp.arange(n, dtype=jnp.int32), axis=0)


def add(*terms):
    total = terms[0].astype(jnp.float32)
    for term in terms[1:]:
        total = total + term.astype(jnp.float32)
    return total.astype(jnp.bfloat16)


def on_device(y_size, tokens, expert_ids, gate_levels, gate_up, down_proj):
    tok_dev, width = tokens.shape
    top = expert_ids.shape[1]
    n = lax.axis_size("expert")
    z_size = n // (2 * y_size)
    me = lax.axis_index("expert")
    core, y, z = me % 2, (me // 2) % y_size, me // (2 * y_size)
    exp_dev = gate_up.shape[0]
    first = me * exp_dev

    gathered = lax.all_gather(tokens, "expert", axis=0, tiled=True)
    gathered = gathered.reshape(z_size, y_size, 2, tok_dev, width)
    small = jnp.concatenate([expert_ids, gate_levels], axis=1).reshape(-1, LANES)
    small = gather_small(small, me, n).reshape(n * tok_dev, 2 * top)
    ids, levels = small[:, :top], small[:, top:].astype(jnp.float32)
    weights = levels / jnp.sum(levels, axis=1, keepdims=True)
    shares = jnp.stack(
        [
            jnp.sum(jnp.where(ids == first + expert, weights, 0.0), axis=1)
            for expert in range(exp_dev)
        ],
        axis=1,
    ).reshape(z_size, y_size, 2, tok_dev, exp_dev)

    def group(y_to, core_to, after):
        at = (0, y_to, core_to, 0, 0)
        rows = lax.dynamic_slice(gathered, at, (z_size, 1, 1, tok_dev, width))
        share = lax.dynamic_slice(shares, at, (z_size, 1, 1, tok_dev, exp_dev))
        rows = rows.reshape(z_size * tok_dev, width)
        share = share.reshape(z_size * tok_dev, exp_dev)
        if after is not None:
            rows, after = lax.optimization_barrier((rows, after))
        part = apply_experts(rows, share, gate_up, down_proj)
        return part, after

    core_pairs = [(i, i ^ 1) for i in range(n)]
    y_pairs = [(i, i ^ 2) for i in range(n)]
    columns = width // CUTS
    from_y = None
    last = None
    for y_to in [(y + step) % y_size for step in range(1, y_size)] + [y]:
        away, last = group(y_to, 1 - core, last)
        arrived = lax.ppermute(away, "expert", core_pairs)
        kept, _ = group(y_to, core, away)
        last = lax.optimization_barrier(kept)
        cuts = [slice(cut * columns, (cut + 1) * columns) for cut in range(CUTS)]
        if y_to is y:
            totals = []
            for cut in range(CUTS):
                terms = [last[:, cuts[cut]], arrived[:, cuts[cut]]]
                totals.append(add(*terms, *([] if from_y is None else [from_y[cut]])))
        else:
            from_y = [
                lax.ppermute(add(last[:, at], arrived[:, at]), "expert", y_pairs) for at in cuts
            ]

    step_z = 2 * y_size
    outs = []
    for cut in range(CUTS):
        own = totals[cut].reshape(z_size, tok_dev, columns)

        def block(at):
            return lax.dynamic_index_in_dim(own, jnp.clip(at, 0, z_size - 1), 0, keepdims=False)

        up, down = None, None
        for step in range(z_size - 1):
            reach = z_size - 1 - step
            up_block, down_block = block(z + reach), block(z - reach)
            up = up_block if up is None else add(up, up_block)
            down = down_block if down is None else add(down, down_block)
            up_pairs = [(i, i + step_z) for i in range(n) if i // step_z + reach < z_size]
            down_pairs = [(i, i - step_z) for i in range(n) if i // step_z >= reach]
            up = lax.ppermute(up, "expert", up_pairs)
            down = lax.ppermute(down, "expert", down_pairs)
        outs.append(add(block(z), up, down) if z_size > 1 else own[0])
    return jnp.concatenate(outs, axis=1)


def solution(mesh):
    y_size = max(1, 4 // mesh.shape["replica"])
    rows = P(("replica", "expert"), None)
    return jax.shard_map(
        functools.partial(on_device, y_size),
        mesh=mesh,
        in_specs=(rows, rows, rows, P("expert", None, None), P("expert", None, None)),
        out_specs=rows,
        check_vma=False,
    )
```

```python
import functools
import jax
import jax.numpy as jnp
from jax import lax
from jax.sharding import PartitionSpec as P

LANES = 128
CUTS = 2


def apply_experts(rows, shares, gate_up, down_proj):
    exp_dev, half, width = down_proj.shape
    parts = []
    for expert in range(exp_dev):
        projected = jnp.dot(rows, gate_up[expert], preferred_element_type=jnp.float32)
        hidden = jax.nn.silu(projected[:, :half]) * projected[:, half:]
        parts.append((hidden * shares[:, expert : expert + 1]).astype(jnp.bfloat16))
    down = down_proj.reshape(exp_dev * half, width)
    return jnp.dot(
        jnp.concatenate(parts, axis=1), down, preferred_element_type=jnp.float32
    ).astype(jnp.bfloat16)


def gather_small(small, me, n):
    held = small[None]
    bit = 1
    while bit < n:
        other = lax.ppermute(held, "expert", [(i, i ^ bit) for i in range(n)])
        held = jnp.concatenate([held, other], axis=0)
        bit *= 2
    return jnp.take(held, me ^ jnp.arange(n, dtype=jnp.int32), axis=0)


def add(*terms):
    total = terms[0].astype(jnp.float32)
    for term in terms[1:]:
        total = total + term.astype(jnp.float32)
    return total.astype(jnp.bfloat16)


def on_device(y_size, tokens, expert_ids, gate_levels, gate_up, down_proj):
    tok_dev, width = tokens.shape
    top = expert_ids.shape[1]
    n = lax.axis_size("expert")
    z_size = n // (2 * y_size)
    me = lax.axis_index("expert")
    core, y, z = me % 2, (me // 2) % y_size, me // (2 * y_size)
    exp_dev = gate_up.shape[0]
    first = me * exp_dev

    small = jnp.concatenate([expert_ids, gate_levels], axis=1).reshape(-1, LANES)
    small = gather_small(small, me, n).reshape(n * tok_dev, 2 * top)
    ids, levels = small[:, :top], small[:, top:].astype(jnp.float32)
    weights = levels / jnp.sum(levels, axis=1, keepdims=True)
    shares = jnp.stack(
        [
            jnp.sum(jnp.where(ids == first + expert, weights, 0.0), axis=1)
            for expert in range(exp_dev)
        ],
        axis=1,
    ).reshape(z_size, y_size, 2, tok_dev, exp_dev)

    core_pairs = [(i, i ^ 1) for i in range(n)]
    y_pairs = [(i, i ^ 2) for i in range(n)]
    step_z = 2 * y_size
    up, down = tokens, tokens
    line = [tokens]
    across = [lax.ppermute(tokens, "expert", y_pairs)] if y_size > 1 else []
    for step in range(1, z_size):
        up = lax.ppermute(up, "expert", [(i, i + step_z) for i in range(n - step_z)])
        down = lax.ppermute(down, "expert", [(i + step_z, i) for i in range(n - step_z)])
        line = [up] + line + [down]
        if y_size > 1:
            have_up = [(i, i ^ 2) for i in range(n) if i // step_z >= step]
            have_down = [(i, i ^ 2) for i in range(n) if i // step_z + step < z_size]
            across = (
                [lax.ppermute(up, "expert", have_up)]
                + across
                + [lax.ppermute(down, "expert", have_down)]
            )

    def assemble(blocks):
        start = (z_size - 1 - z) * tok_dev
        return lax.dynamic_slice_in_dim(
            jnp.concatenate(blocks, axis=0), start, z_size * tok_dev, axis=0
        )

    own_line = assemble(line)
    lines = {0: (own_line, lax.ppermute(own_line, "expert", core_pairs))}

    def group(y_step, core_step, after):
        at = (0, (y + y_step) % y_size, (core + core_step) % 2, 0, 0)
        rows = lines[y_step][core_step]
        share = lax.dynamic_slice(shares, at, (z_size, 1, 1, tok_dev, exp_dev))
        share = share.reshape(z_size * tok_dev, exp_dev)
        if after is not None:
            rows, after = lax.optimization_barrier((rows, after))
        part = apply_experts(rows, share, gate_up, down_proj)
        return part, after

    columns = width // CUTS
    cuts = [slice(cut * columns, (cut + 1) * columns) for cut in range(CUTS)]
    kept_own, _ = group(0, 0, None)
    last = kept_own
    from_y = None
    if y_size > 1:
        across, kept_own = lax.optimization_barrier((across, kept_own))
        other = assemble(across)
        lines[1] = (other, lax.ppermute(other, "expert", core_pairs))
        away, kept_own = group(1, 1, kept_own)
        arrived = lax.ppermute(away, "expert", core_pairs)
        kept, _ = group(1, 0, away)
        kept = lax.optimization_barrier(kept)
        last = [add(kept[:, at], arrived[:, at]) for at in cuts]
        from_y = [lax.ppermute(part, "expert", y_pairs) for part in last]
        away, from_y[0] = group(0, 1, from_y[0])
    else:
        away, kept_own = group(0, 1, kept_own)
    arrived = lax.ppermute(away, "expert", core_pairs)
    totals = []
    for cut, at in enumerate(cuts):
        terms = [kept_own[:, at], arrived[:, at]]
        totals.append(add(*terms, *([] if from_y is None else [from_y[cut]])))

    outs = []
    for cut in range(CUTS):
        own = totals[cut].reshape(z_size, tok_dev, columns)

        def block(at):
            return lax.dynamic_index_in_dim(own, jnp.clip(at, 0, z_size - 1), 0, keepdims=False)

        up, down = None, None
        for step in range(z_size - 1):
            reach = z_size - 1 - step
            up_block, down_block = block(z + reach), block(z - reach)
            up = up_block if up is None else add(up, up_block)
            down = down_block if down is None else add(down, down_block)
            up_pairs = [(i, i + step_z) for i in range(n) if i // step_z + reach < z_size]
            down_pairs = [(i, i - step_z) for i in range(n) if i // step_z >= reach]
            up = lax.ppermute(up, "expert", up_pairs)
            down = lax.ppermute(down, "expert", down_pairs)
        outs.append(add(block(z), up, down) if z_size > 1 else own[0])
    return jnp.concatenate(outs, axis=1)


def solution(mesh):
    y_size = max(1, 4 // mesh.shape["replica"])
    rows = P(("replica", "expert"), None)
    return jax.shard_map(
        functools.partial(on_device, y_size),
        mesh=mesh,
        in_specs=(rows, rows, rows, P("expert", None, None), P("expert", None, None)),
        out_specs=rows,
        check_vma=False,
    )
```
